32 devices in a mesh: grp: 4 (over y, core), seq: 8 (over z, x).
Axes of the slice: x: 2, y: 2, z: 4, core: 2. Of those that a mesh axis runs over, the one named last changes fastest.
Arguments:
- query_heads: bfloat16 [32, 12, 128, 128], P('grp', None, 'seq'), may hold values from -40 to 40
- key_heads: bfloat16 [32, 12, 128, 128], P('grp', None, 'seq'), may hold values from -40 to 40
- value_heads: bfloat16 [32, 12, 128, 128], P('grp', None, 'seq'), may hold values from -8 to 8
- residual: bfloat16 [32, 128, 1536], P('grp', 'seq'), may hold values from -16 to 16
- modulation: bfloat16 [32, 4, 1536], P('grp'), may hold values from 0.099609375 to 1.8984375
- router: bfloat16 [1536, 8], replicated, may hold values from -0.15625 to 0.15625
- up_proj: bfloat16 [8, 2048, 1536], P('seq', 'grp'), may hold values from -0.15625 to 0.15625
- down_proj: bfloat16 [8, 2048, 1536], P('seq', 'grp'), may hold values from -0.125 to 0.125
- expert_ids: int32 [4, 8, 128, 2], P('grp', 'seq'), may hold values from 0 to 7, all different within a row; in each aligned block of 128 rows (0 to 127, 128 to 255, ..., all dimensions but the last counted through in order) at most 64 rows name the same one
Outputs:
- output: bfloat16 [32, 128, 1536], P('grp', 'seq')
The draws below stay inside these ranges and needn't reach their ends.
Inputs may be any that keep to these rules, and one draw needn't show every extreme that they name: `expert_ids`: each token names two different experts. Among the 128 tokens of one device no expert is named by more than 64 of them, and in every draw some device names some expert exactly 64 times.
All inputs are finite; a program needn't handle non-finite values.
Results may differ from the reference program's by a relative error of at most 0.012.
Values may be sent and summed in bfloat16 or wider, within the bound.
A program may use at most 64 MiB of HBM per device.

```python
import math
import jax
import jax.numpy as jnp
import numpy as np
from jax import lax

HEAD_DIM = 128
HEADS = 12
D = 1536
FF = 2048
SEQS = 8
LD = 16
EXPERTS = 8
TOK_DEV = 128
LENGTH = 128
BATCH = 32
C = 64
N_GRP = 4
N_SEQ = 8


def paired_fields(key):
    dims_all = (BATCH, HEADS, LENGTH, HEAD_DIM)
    return dims_all


def draw_query_heads(key, part):
    dims_all = paired_fields(key)
    key = jax.random.fold_in(key, 1)
    field = 1.3 * jax.random.normal(key, dims_all, jnp.float32)
    return jnp.clip(field, -40.0, 40.0).astype(jnp.bfloat16)


def draw_key_heads(key, part):
    dims_all = paired_fields(key)
    key = jax.random.fold_in(key, 2)
    field = 1.3 * jax.random.normal(key, dims_all, jnp.float32)
    return jnp.clip(field, -40.0, 40.0).astype(jnp.bfloat16)


def draw_residual(key, part):
    key = jax.random.fold_in(key, 3)
    dims_all = (BATCH, LENGTH, D)
    field = jax.random.normal(key, dims_all, jnp.float32)
    return jnp.clip(field, -16.0, 16.0).astype(jnp.bfloat16)


def block_levels(stream_key, dims, shards, smallest, high):
    level = 1.0
    for dim, parts in shards:
        steps = jax.random.uniform(jax.random.fold_in(jax.random.fold_in(stream_key, 6), dim), (parts,), jnp.float32, smallest / len(shards), high / len(shards))
        level = level * jnp.repeat(jnp.exp(steps), dims[dim] // parts).reshape((-1,) + (1,) * (len(dims) - 1 - dim))
    return level


def routed_block(own_key, own, number, rows, amount, top, limit, skew):
    sequence = jax.random.permutation(own_key, amount)
    crowded, usual = shares(amount, rows * top, limit, skew, True), shares(amount, rows * top, limit, skew, False)
    places = jnp.arange(amount)

    def named(lengths, offset_by):
        used = int((lengths > 0).sum())
        fixed = max(1, used // 4)
        moved = fixed + (places - fixed + offset_by * (used - fixed)) % max(1, amount - fixed)
        return jnp.zeros((amount,), jnp.int32).at[sequence[jnp.where(places < fixed, places, moved)]].set(jnp.asarray(lengths, jnp.int32))

    lengths = jnp.where(number % 4 == 0, named(crowded, number // 4), named(usual, number - number // 4 - 1))
    mixed = jax.random.permutation(jax.random.fold_in(own, 3), amount)
    source_of, taker = mixed[0:amount // 2 * 2:2], mixed[1:amount // 2 * 2:2]
    room = jnp.minimum(lengths[source_of] - 1, limit - lengths[taker]) // 2
    room = jnp.where((source_of == sequence[0]) | (taker == sequence[0]) | (lengths[taker] == 0), 0, jnp.maximum(room, 0))
    moved = jax.random.randint(jax.random.fold_in(own, 4), (amount // 2,), 0, 1 << 20) % (room + 1)
    lengths = lengths.at[source_of].add(-moved).at[taker].add(moved)
    items = jnp.searchsorted(jnp.cumsum(lengths), jnp.arange(rows * top), side="right").astype(jnp.int32)
    grid = items.reshape(top, rows).T
    grid = grid[jax.random.permutation(jax.random.fold_in(own, 1), rows)]
    offset_by = jax.random.randint(jax.random.fold_in(own, 2), (rows, 1), 0, top)
    return jnp.take_along_axis(grid, (jnp.arange(top)[None, :] + offset_by) % top, axis=1)


def shares(count, total, limit, skew, full):
    loads = [(1 << 20) // math.isqrt(grade ** skew) + 1 for grade in range(1, count + 1)]
    largest = limit if full else min(limit, max(-(-total // count), total * loads[0] // sum(loads)))
    least = 1 if total - largest >= count - 1 else 0
    holding, surplus = [largest] + [least] * (count - 1), total - largest - least * (count - 1)
    while surplus > 0:
        movable = [i for i in range(1, count) if holding[i] < largest] or [i for i in range(1, count) if holding[i] < limit]
        whole, remaining = sum([loads[i] for i in movable]), surplus
        for i in movable:
            addition = min(limit - holding[i], max(1, remaining * loads[i] // whole), surplus)
            holding[i] = holding[i] + addition
            surplus = surplus - addition
    return np.array(holding)


def normal_values(own_key, dims, width, reach, cuts=(), kind=jnp.bfloat16):
    gain = block_levels(own_key, dims, cuts, -0.22, 0.18) if cuts else 1.0
    entries = jax.random.normal(own_key, dims, jnp.float32) * width * gain
    return jnp.minimum(jnp.maximum(entries, -reach), reach).astype(kind)


def setup_inputs(seed: int = 0) -> dict:
    key_list = jax.random.split(jax.random.key(seed), 10)
    query_heads = draw_query_heads(jax.random.fold_in(key_list[9], 71), 0)
    key_heads = draw_key_heads(jax.random.fold_in(key_list[9], 71), 0)
    value_heads = normal_values(key_list[2], (BATCH, HEADS, LENGTH, HEAD_DIM), 2.0, 8.0, ((0, 4), (2, 8)))
    residual = draw_residual(jax.random.fold_in(key_list[9], 71), 0)
    modulation = jnp.clip(1.0 + 0.18 * jax.random.normal(key_list[4], (BATCH, 4, D), jnp.float32), 0.099609375, 1.8984375).astype(jnp.bfloat16)
    router = normal_values(key_list[5], (D, EXPERTS), D ** -0.5, 0.15625)
    up_proj = normal_values(key_list[6], (EXPERTS, FF, D), D ** -0.5, 0.15625, ((0, 8), (1, 4)))
    down_proj = normal_values(key_list[7], (EXPERTS, FF, D), FF ** -0.5, 0.125, ((0, 8), (1, 4)))
    expert_ids_keys = jax.random.split(jax.random.fold_in(key_list[8], 1), N_GRP * N_SEQ * TOK_DEV // TOK_DEV)
    expert_ids_turns = jax.random.permutation(jax.random.fold_in(key_list[8], 3), N_GRP * N_SEQ * TOK_DEV // TOK_DEV)
    expert_ids = jax.vmap(lambda own, number: routed_block(jax.random.fold_in(key_list[8], 2), own, number, TOK_DEV, EXPERTS, 2, C, 2))(expert_ids_keys, expert_ids_turns).reshape((N_GRP, N_SEQ, TOK_DEV, 2))
    return {"query_heads": query_heads, "key_heads": key_heads, "value_heads": value_heads, "residual": residual, "modulation": modulation, "router": router, "up_proj": up_proj, "down_proj": down_proj, "expert_ids": expert_ids}


norm_eps = 1e-06

def attend_sequence(pieces):
    single_query_rows, single_key_rows, single_value_rows = pieces
    scale_factor_term = 1.0 / math.sqrt(single_query_rows.shape[-1])
    attention_scores = jnp.einsum('nrf,njf->nrj', single_query_rows.astype(jnp.float32), single_key_rows.astype(jnp.float32)) * scale_factor_term
    weight_matrix_set = jax.nn.softmax(attention_scores, axis=-1).astype(jnp.bfloat16)
    return jnp.einsum('xob,xbp->xop', weight_matrix_set.astype(jnp.float32), single_value_rows.astype(jnp.float32)).astype(jnp.bfloat16)

def reference(query_heads, key_heads, value_heads, residual, modulation, router, up_proj, down_proj, expert_ids):
    batch_size, head_count, length, head_width = query_heads.shape
    model_width = head_count * head_width
    attended = lax.map(attend_sequence, (query_heads, key_heads, value_heads))
    attn_tok = attended.transpose(0, 2, 1, 3).reshape(batch_size, length, model_width)
    modulators = modulation.astype(jnp.float32)
    stream = (residual.astype(jnp.float32) + modulators[:, 0:1, :] * attn_tok.astype(jnp.float32)).astype(jnp.bfloat16)
    widened = stream.astype(jnp.float32)
    center = lax.optimization_barrier(jnp.mean(widened, axis=-1, keepdims=True))
    spread = lax.optimization_barrier(jnp.mean(jnp.square(widened - center), axis=-1, keepdims=True))
    normed = ((widened - center) * lax.rsqrt(spread + norm_eps) * modulators[:, 1:2, :] + modulators[:, 2:3, :]).astype(jnp.bfloat16)
    token_count = batch_size * length
    tokens = normed.reshape(token_count, model_width)
    chosen = expert_ids.reshape(N_GRP, N_SEQ, SEQS, LD, 2).transpose(0, 2, 1, 3, 4).reshape(token_count, 2).astype(jnp.int32)
    logits = jnp.dot(tokens, router, preferred_element_type=jnp.float32)
    picked = jnp.take_along_axis(logits, chosen, axis=1)
    lifted = jax.nn.sigmoid(picked)
    gate_mix = lifted / lax.optimization_barrier(jnp.sum(lifted, axis=1, keepdims=True))
    experts = router.shape[1]
    assign_expert = chosen.reshape(-1)
    assign_token = (jnp.arange(token_count * 2, dtype=jnp.int32) // 2).astype(jnp.int32)
    assign_gate = gate_mix.reshape(-1)
    sorted_ids = jnp.argsort(assign_expert, stable=True).astype(jnp.int32)
    counts = lax.optimization_barrier(jnp.sum((assign_expert[:, None] == jnp.arange(experts, dtype=jnp.int32)[None, :]).astype(jnp.int32), axis=0))
    offsets = (jnp.cumsum(counts) - counts).astype(jnp.int32)
    block_rows = 512
    padded_ids = jnp.concatenate([sorted_ids, jnp.zeros((block_rows,), jnp.int32)])

    def one_expert(running, expert_index):
        up_mat = up_proj[expert_index]
        down_mat = down_proj[expert_index]
        first_row = offsets[expert_index]
        live_count = counts[expert_index]

        def one_block(block_step, inner_total):
            row_begin = (first_row + block_step * block_rows).astype(jnp.int32)
            picked_rows = lax.dynamic_slice(padded_ids, (row_begin,), (block_rows,))
            active_flag = block_step * block_rows + jnp.arange(block_rows, dtype=jnp.int32) < live_count
            token_index = assign_token[picked_rows]
            gathered = tokens[token_index]
            pre_act = lax.dot_general(gathered, up_mat, (((1,), (1,)), ((), ())), preferred_element_type=jnp.float32)
            hidden = jax.nn.gelu(pre_act).astype(jnp.bfloat16)
            result = jnp.dot(hidden, down_mat, preferred_element_type=jnp.float32).astype(jnp.bfloat16)
            weight = jnp.where(active_flag, assign_gate[picked_rows], jnp.zeros_like(assign_gate[picked_rows]))
            return inner_total.at[token_index].add(weight[:, None] * result.astype(jnp.float32))
        block_total = ((live_count + block_rows - 1) // block_rows).astype(jnp.int32)
        running = lax.fori_loop(jnp.int32(0), block_total, one_block, running)
        return (running, None)
    moe_sum, _ = lax.scan(one_expert, jnp.zeros((token_count, model_width), jnp.float32), jnp.arange(experts, dtype=jnp.int32))
    moe_sum = moe_sum.reshape(batch_size, length, model_width)
    return (widened + modulators[:, 3:4, :] * moe_sum).astype(jnp.bfloat16)
```

```python
import functools
import math

import jax
import jax.numpy as jnp
from jax import lax
from jax.experimental import pallas as pl
from jax.experimental.pallas import tpu as pltpu
from jax.sharding import PartitionSpec as P

norm_eps = 1e-06
BF = jnp.bfloat16
F32 = jnp.float32


def wait_bytes(ref, sem):
    pltpu.make_async_copy(ref, ref, sem).wait()


def remote(src, dst, send_sem, recv_sem, axis, index):
    return pltpu.make_async_remote_copy(
        src_ref=src,
        dst_ref=dst,
        send_sem=send_sem,
        recv_sem=recv_sem,
        device_id={axis: index},
        device_id_type=pl.DeviceIdType.MESH,
    )


def layer_kernel(
    n, n_grp, chunks,
    q_ref, k_ref, v_ref, res_ref, mod_ref, router_ref, up_ref, down_ref, ids_ref, idst_ref,
    out_ref,
    qkv, o_buf, att, stream, normed, slot_t, mix, outb, arr, back, weights, acc, moe,
    q_send, q_recv, a_send, a_recv, d_send, d_recv, r_send, r_recv,
    w_local, w_send, w_peer, w_sib, f_send, f_recv,
):
    me = lax.axis_index("seq")
    grp = lax.axis_index("grp")
    sib = grp + 1 - 2 * (grp % 2)
    chips = n_grp // 2
    half = n // 2
    seqs, ld, width = res_ref.shape
    pc = q_ref.shape[1]
    hd = q_ref.shape[3]
    heads = width // hd
    part = pc // chunks
    tok = seqs * ld
    cap = outb.shape[1]
    ff = weights.shape[2]
    fh = ff // 2

    def other(t):
        return (me + 1 + (half - 1 + t) % (n - 1)) % n

    def peer(t):
        return (grp + 2 * (t + 1)) % n_grp

    barrier = pltpu.get_barrier_semaphore()
    for t in range(n - 1):
        pl.semaphore_signal(
            barrier, inc=1, device_id={"seq": other(t)}, device_id_type=pl.DeviceIdType.MESH
        )
    for t in range(chips - 1):
        pl.semaphore_signal(
            barrier, inc=1, device_id={"grp": peer(t)}, device_id_type=pl.DeviceIdType.MESH
        )
    pl.semaphore_signal(barrier, inc=1, device_id={"grp": sib}, device_id_type=pl.DeviceIdType.MESH)
    pl.semaphore_wait(barrier, n - 1 + chips)

    def send_chunk(c):
        pairs = pl.ds(c * part, part)
        mine = pl.ds(pl.multiple_of(me * ld, ld), ld)

        def send_to(t, carry):
            dst = other(t)
            for i, ref in enumerate((q_ref, k_ref, v_ref)):
                remote(
                    ref.at[dst, pairs], qkv.at[i, pairs, mine], q_send, q_recv.at[c], "seq", dst
                ).start()
            return carry

        lax.fori_loop(0, n - 1, send_to, 0)
        for i, ref in enumerate((q_ref, k_ref, v_ref)):
            pltpu.make_async_copy(ref.at[me, pairs], qkv.at[i, pairs, mine], q_recv.at[c]).start()

    send_chunk(0)

    pieces = [(i, pl.ds(r * fh, fh)) for i in range(2) for r in range(2)]
    sources = (up_ref, down_ref)
    for j, (i, rows) in enumerate(pieces):
        for t in range(chips - 1):
            remote(
                sources[i].at[0, rows], weights.at[i, grp, rows], w_send,
                w_peer.at[grp // 2, j], "grp", peer(t),
            ).start()
    for c in range(1, chunks):
        send_chunk(c)
    for i in range(2):
        pltpu.make_async_copy(sources[i].at[0], weights.at[i, grp], w_local).start()
        remote(sources[i].at[0], weights.at[i, grp], w_send, w_sib, "grp", sib).start()

    experts = n
    before = (
        lax.broadcasted_iota(jnp.int32, (tok, tok), 0)
        < lax.broadcasted_iota(jnp.int32, (tok, tok), 1)
    ).astype(F32)
    row_e = lax.broadcasted_iota(jnp.int32, (experts, tok), 0)
    named_t = ((row_e == idst_ref[0:1, :]) | (row_e == idst_ref[1:2, :])).astype(F32)
    rank_t = jnp.dot(named_t, before, preferred_element_type=F32)
    slot_t[...] = jnp.where(named_t > 0.0, rank_t, -1.0)

    scale = 1.0 / math.sqrt(hd)

    def attend(c, carry):
        pairs = pl.ds(c * part, part)
        wait_bytes(qkv.at[:, pairs], q_recv.at[c])
        for i in range(part):
            p = c * part + i
            s = lax.dot_general(
                qkv[0, p], qkv[1, p], (((1,), (1,)), ((), ())), preferred_element_type=F32
            )
            s = s * scale
            e = jnp.exp(s - jnp.max(s, axis=-1, keepdims=True))
            wts = (e / jnp.sum(e, axis=-1, keepdims=True)).astype(BF)
            o_buf[p] = jnp.dot(wts, qkv[2, p], preferred_element_type=F32).astype(BF)
        there = pl.ds(me * pc + c * part, part)

        def send_to(t, carry2):
            dst = other(t)
            rows = pl.ds(pl.multiple_of(dst * ld, ld), ld)
            remote(o_buf.at[pairs, rows], att.at[there], a_send, a_recv, "seq", dst).start()
            return carry2

        lax.fori_loop(0, n - 1, send_to, 0)
        mine = pl.ds(pl.multiple_of(me * ld, ld), ld)
        att[there] = o_buf[pairs, mine]
        return carry

    lax.fori_loop(0, chunks, attend, 0)
    wait_bytes(att.at[pl.ds(0, (n - 1) * pc)], a_recv)

    def normalise(b, carry):
        row = jnp.concatenate([att[b * heads + h] for h in range(heads)], axis=-1)
        m = mod_ref[b].astype(F32)
        st = (res_ref[b].astype(F32) + m[0:1] * row.astype(F32)).astype(BF)
        stream[b] = st
        x = st.astype(F32)
        center = jnp.mean(x, axis=-1, keepdims=True)
        d = x - center
        spread = jnp.mean(d * d, axis=-1, keepdims=True)
        normed[b] = (d * lax.rsqrt(spread + norm_eps) * m[1:2] + m[2:3]).astype(BF)
        return carry

    lax.fori_loop(0, seqs, normalise, 0)
    tokens = normed[...].reshape(tok, width)

    def pack(e):
        place = lax.broadcasted_iota(jnp.int32, (cap, tok), 0).astype(F32)
        hot = (place == slot_t[pl.ds(e, 1), :]).astype(BF)
        return jnp.dot(hot, normed[...].reshape(tok, width), preferred_element_type=F32).astype(BF)

    def dispatch(t, carry):
        dst = other(t)
        outb[dst] = pack(dst)
        remote(outb.at[dst], arr.at[me], d_send, d_recv.at[me // half], "seq", dst).start()
        return carry

    lax.fori_loop(0, n - 1, dispatch, 0)
    arr[me] = pack(me)

    after = (
        lax.broadcasted_iota(jnp.int32, (tok, tok), 1)
        < lax.broadcasted_iota(jnp.int32, (tok, tok), 0)
    ).astype(F32)
    col_e = lax.broadcasted_iota(jnp.int32, (tok, experts), 1)
    named = ((col_e == ids_ref[:, 0:1]) | (col_e == ids_ref[:, 1:2])).astype(F32)
    slot = jnp.where(named > 0.0, jnp.dot(after, named, preferred_element_type=F32), -1.0)
    logits = jnp.dot(tokens, router_ref[...], preferred_element_type=F32)
    lifted = jnp.where(named > 0.0, jax.nn.sigmoid(logits), 0.0)
    gate = lifted / jnp.sum(lifted, axis=1, keepdims=True)
    gate_hi = gate.astype(BF)
    gate_lo = (gate - gate_hi.astype(F32)).astype(BF)
    rows_all = experts * cap
    wide = lax.broadcasted_iota(jnp.int32, (experts, rows_all), 1)
    first = lax.broadcasted_iota(jnp.int32, (experts, rows_all), 0) * cap
    spread_e = ((wide >= first) & (wide < first + cap)).astype(BF)
    slot_all = jnp.dot(slot.astype(BF), spread_e, preferred_element_type=F32)
    place_all = (lax.broadcasted_iota(jnp.int32, (tok, rows_all), 1) % cap).astype(F32)
    here = slot_all == place_all
    hi_all = jnp.dot(gate_hi, spread_e, preferred_element_type=F32)
    lo_all = jnp.dot(gate_lo, spread_e, preferred_element_type=F32)
    mix[0] = jnp.where(here, hi_all, 0.0).astype(BF)
    mix[1] = jnp.where(here, lo_all, 0.0).astype(BF)

    for j, (i, rows) in enumerate(pieces):
        for t in range(chips - 1):
            g = peer(t)
            wait_bytes(weights.at[i, g, rows], w_peer.at[g // 2, j])
            piece = weights.at[i, g, rows]
            remote(piece, piece, f_send, f_recv, "grp", sib).start()
    for i in range(2):
        wait_bytes(weights.at[i, grp], w_local)
    wait_bytes(weights.at[:, pl.ds(0, 1)], w_sib)
    wait_bytes(weights.at[:, pl.ds(0, chips - 1)], f_recv)

    my_half = me // half
    far = 1 - my_half
    wait_bytes(arr.at[pl.ds(0, half)], d_recv.at[far])
    for step in range(2):
        side = far if step == 0 else my_half
        if step == 1:
            wait_bytes(arr.at[pl.ds(0, half - 1)], d_recv.at[my_half])
        block = pl.ds(side * half, half)

        def expert(g, carry, block=block):
            x = arr[block].reshape(half * cap, width)
            u = lax.dot_general(
                x, weights[0, g], (((1,), (1,)), ((), ())), preferred_element_type=F32
            )
            inner = math.sqrt(2.0 / math.pi) * (u + 0.044715 * (u * u * u))
            hidden = (0.5 * u * (1.0 + jnp.tanh(inner))).astype(BF)
            add = jnp.dot(hidden, weights[1, g], preferred_element_type=F32)
            acc[...] = jnp.where(g == 0, add, acc[...] + add)
            return carry

        acc[...] = jnp.zeros_like(acc)
        lax.fori_loop(0, n_grp, expert, 0)
        outcome = acc[...].astype(BF).reshape(half, cap, width)
        arr[block] = outcome
        for i in range(half):
            dst = side * half + (me + i) % half

            def go(dst=dst):
                remote(
                    arr.at[dst], back.at[me], r_send, r_recv.at[my_half], "seq", dst
                ).start()

            if step == 0:
                go()
            elif i > 0:
                go()
            else:
                back[me] = arr[me]

    for step in range(2):
        side = my_half if step == 0 else far
        count = half - 1 if step == 0 else half
        wait_bytes(back.at[pl.ds(0, count)], r_recv.at[side])
        rows = back[pl.ds(side * half, half)].reshape(half * cap, width)
        lanes = pl.ds(pl.multiple_of(side * (half * cap), half * cap), half * cap)
        add = jnp.dot(mix[0, :, lanes], rows, preferred_element_type=F32)
        add = add + jnp.dot(mix[1, :, lanes], rows, preferred_element_type=F32)
        moe[...] = add if step == 0 else moe[...] + add

    def finish(b, carry):
        m = mod_ref[b].astype(F32)
        rows = moe[pl.ds(pl.multiple_of(b * ld, ld), ld), :]
        out_ref[b] = (stream[b].astype(F32) + m[3:4] * rows).astype(BF)
        return carry

    lax.fori_loop(0, seqs, finish, 0)

    wait_bytes(qkv.at[:, :, pl.ds(0, (n - 1) * ld)], q_send)
    wait_bytes(att.at[pl.ds(0, (n - 1) * pc)], a_send)
    wait_bytes(outb.at[pl.ds(0, n - 1)], d_send)
    wait_bytes(back.at[pl.ds(0, n - 1)], r_send)
    wait_bytes(weights.at[:, pl.ds(0, chips)], w_send)
    wait_bytes(weights.at[:, pl.ds(0, chips - 1)], f_send)


def per_device(
    query_heads, key_heads, value_heads, residual, modulation, router, up_proj, down_proj,
    expert_ids,
):
    seqs, heads, ld, hd = query_heads.shape
    n = lax.axis_size("seq")
    n_grp = lax.axis_size("grp")
    pc = seqs * heads // n
    chunks = 3 if pc % 3 == 0 else 1
    tok = seqs * ld
    width = heads * hd
    experts = router.shape[1]
    cap = 4 * tok // experts
    ff = up_proj.shape[1]
    half = n // 2

    def arrange(array):
        return array.reshape(n, pc, ld, hd)

    ids = expert_ids.reshape(tok, 2)
    any_spec = pl.BlockSpec(memory_space=pl.ANY)
    vmem = pl.BlockSpec(memory_space=pltpu.VMEM)
    dma = pltpu.SemaphoreType.DMA
    return pl.pallas_call(
        functools.partial(layer_kernel, n, n_grp, chunks),
        out_shape=jax.ShapeDtypeStruct((seqs, ld, width), BF),
        in_specs=[any_spec] * 3 + [vmem] * 3 + [any_spec] * 2 + [vmem] * 2,
        out_specs=vmem,
        scratch_shapes=[
            pltpu.VMEM((3, pc, n * ld, hd), BF),
            pltpu.VMEM((pc, n * ld, hd), BF),
            pltpu.VMEM((n * pc, ld, hd), BF),
            pltpu.VMEM((seqs, ld, width), BF),
            pltpu.VMEM((seqs, ld, width), BF),
            pltpu.VMEM((experts, tok), F32),
            pltpu.VMEM((2, tok, experts * cap), BF),
            pltpu.VMEM((n, cap, width), BF),
            pltpu.VMEM((n, cap, width), BF),
            pltpu.VMEM((n, cap, width), BF),
            pltpu.VMEM((2, n_grp, ff, width), BF),
            pltpu.VMEM((half * cap, width), F32),
            pltpu.VMEM((tok, width), F32),
            dma, dma((chunks,)), dma, dma, dma, dma((2,)), dma, dma((2,)),
            dma, dma, dma((n_grp // 2, 4)), dma, dma, dma,
        ],
        compiler_params=pltpu.CompilerParams(
            collective_id=0, has_side_effects=True, vmem_limit_bytes=52 * 1024 * 1024
        ),
    )(
        arrange(query_heads), arrange(key_heads), arrange(value_heads), residual, modulation,
        router, up_proj, down_proj, ids, ids.T,
    )


def solution(mesh):
    return jax.shard_map(
        per_device,
        mesh=mesh,
        in_specs=(
            P("grp", None, "seq", None),
            P("grp", None, "seq", None),
            P("grp", None, "seq", None),
            P("grp", "seq", None),
            P("grp", None, None),
            P(),
            P("seq", "grp", None),
            P("seq", "grp", None),
            P("grp", "seq", None, None),
        ),
        out_specs=P("grp", "seq", None),
        check_vma=False,
    )
```

```python
import functools
import math

import jax
import jax.numpy as jnp
from jax import lax
from jax.experimental import pallas as pl
from jax.experimental.pallas import tpu as pltpu
from jax.sharding import PartitionSpec as P

norm_eps = 1e-06
BF = jnp.bfloat16
F32 = jnp.float32


def wait_bytes(ref, sem):
    pltpu.make_async_copy(ref, ref, sem).wait()


def remote(src, dst, send_sem, recv_sem, axis, index):
    return pltpu.make_async_remote_copy(
        src_ref=src,
        dst_ref=dst,
        send_sem=send_sem,
        recv_sem=recv_sem,
        device_id={axis: index},
        device_id_type=pl.DeviceIdType.MESH,
    )


def layer_kernel(
    n, n_grp, chunks,
    q_ref, k_ref, v_ref, res_ref, mod_ref, router_ref, up_ref, down_ref, idst_ref,
    out_ref,
    resid, qkv, o_buf, att, stream, normed, slot_t, mix, outb, arr, back, weights, acc, moe,
    q_send, q_recv, a_send, a_recv, d_send, d_recv, r_send, r_recv,
    w_local, w_send, w_peer, w_sib, f_send, f_recv, res_sem,
):
    me = lax.axis_index("seq")
    grp = lax.axis_index("grp")
    sib = grp + 1 - 2 * (grp % 2)
    chips = n_grp // 2
    half = n // 2
    seqs, ld, width = res_ref.shape
    pc = q_ref.shape[1]
    hd = q_ref.shape[3]
    heads = width // hd
    part = pc // chunks
    tok = seqs * ld
    cap = outb.shape[1]
    ff = weights.shape[2]
    fh = ff // 2

    def other(t):
        return (me + 1 + (half - 1 + t) % (n - 1)) % n

    def peer(t):
        return (grp + 2 * (t + 1)) % n_grp

    barrier = pltpu.get_barrier_semaphore()
    for t in range(n - 1):
        pl.semaphore_signal(
            barrier, inc=1, device_id={"seq": other(t)}, device_id_type=pl.DeviceIdType.MESH
        )
    for t in range(chips - 1):
        pl.semaphore_signal(
            barrier, inc=1, device_id={"grp": peer(t)}, device_id_type=pl.DeviceIdType.MESH
        )
    pl.semaphore_signal(barrier, inc=1, device_id={"grp": sib}, device_id_type=pl.DeviceIdType.MESH)
    pl.semaphore_wait(barrier, n - 1 + chips)

    def send_chunk(c):
        pairs = pl.ds(c * part, part)
        mine = pl.ds(pl.multiple_of(me * ld, ld), ld)

        def send_to(t, carry):
            dst = other(t)
            for i, ref in enumerate((q_ref, k_ref, v_ref)):
                remote(
                    ref.at[dst, pairs], qkv.at[i, pairs, mine], q_send, q_recv.at[c], "seq", dst
                ).start()
            return carry

        lax.fori_loop(0, n - 1, send_to, 0)
        for i, ref in enumerate((q_ref, k_ref, v_ref)):
            pltpu.make_async_copy(ref.at[me, pairs], qkv.at[i, pairs, mine], q_recv.at[c]).start()

    send_chunk(0)

    pieces = [(i, pl.ds(r * fh, fh)) for i in range(2) for r in range(2)]
    sources = (up_ref, down_ref)
    for j, (i, rows) in enumerate(pieces):
        for t in range(chips - 1):
            remote(
                sources[i].at[0, rows], weights.at[i, grp, rows], w_send,
                w_peer.at[grp // 2, j], "grp", peer(t),
            ).start()
    for c in range(1, chunks):
        send_chunk(c)
    for i in range(2):
        pltpu.make_async_copy(sources[i].at[0], weights.at[i, grp], w_local).start()
        remote(sources[i].at[0], weights.at[i, grp], w_send, w_sib, "grp", sib).start()

    pltpu.make_async_copy(res_ref, resid, res_sem).start()

    experts = n
    before = (
        lax.broadcasted_iota(jnp.int32, (tok, tok), 0)
        < lax.broadcasted_iota(jnp.int32, (tok, tok), 1)
    ).astype(F32)
    row_e = lax.broadcasted_iota(jnp.int32, (experts, tok), 0)
    named_t = ((row_e == idst_ref[0:1, :]) | (row_e == idst_ref[1:2, :])).astype(F32)
    rank_t = jnp.dot(named_t, before, preferred_element_type=F32)
    slot_t[...] = jnp.where(named_t > 0.0, rank_t, -1.0)

    scale = 1.0 / math.sqrt(hd)

    def attend(c, carry):
        pairs = pl.ds(c * part, part)
        wait_bytes(qkv.at[:, pairs], q_recv.at[c])
        for i in range(part):
            p = c * part + i
            s = lax.dot_general(
                qkv[0, p], qkv[1, p], (((1,), (1,)), ((), ())), preferred_element_type=F32
            )
            s = s * scale
            e = jnp.exp(s - jnp.max(s, axis=-1, keepdims=True))
            wts = (e / jnp.sum(e, axis=-1, keepdims=True)).astype(BF)
            o_buf[p] = jnp.dot(wts, qkv[2, p], preferred_element_type=F32).astype(BF)
        there = pl.ds(me * pc + c * part, part)

        def send_to(t, carry2):
            dst = other(t)
            rows = pl.ds(pl.multiple_of(dst * ld, ld), ld)
            remote(o_buf.at[pairs, rows], att.at[there], a_send, a_recv, "seq", dst).start()
            return carry2

        lax.fori_loop(0, n - 1, send_to, 0)
        mine = pl.ds(pl.multiple_of(me * ld, ld), ld)
        att[there] = o_buf[pairs, mine]
        return carry

    lax.fori_loop(0, chunks, attend, 0)
    wait_bytes(att.at[pl.ds(0, (n - 1) * pc)], a_recv)

    wait_bytes(resid, res_sem)
    def normalise(b, carry):
        row = jnp.concatenate([att[b * heads + h] for h in range(heads)], axis=-1)
        m = mod_ref[b].astype(F32)
        st = (resid[b].astype(F32) + m[0:1] * row.astype(F32)).astype(BF)
        stream[b] = st
        x = st.astype(F32)
        center = jnp.mean(x, axis=-1, keepdims=True)
        d = x - center
        spread = jnp.mean(d * d, axis=-1, keepdims=True)
        normed[b] = (d * lax.rsqrt(spread + norm_eps) * m[1:2] + m[2:3]).astype(BF)
        return carry

    lax.fori_loop(0, seqs, normalise, 0)
    tokens = normed[...].reshape(tok, width)

    def pack(e):
        place = lax.broadcasted_iota(jnp.int32, (cap, tok), 0).astype(F32)
        hot = (place == slot_t[pl.ds(e, 1), :]).astype(BF)
        return jnp.dot(hot, normed[...].reshape(tok, width), preferred_element_type=F32).astype(BF)

    def dispatch(t, carry):
        dst = other(t)
        outb[dst] = pack(dst)
        remote(outb.at[dst], arr.at[me], d_send, d_recv.at[me // half], "seq", dst).start()
        return carry

    lax.fori_loop(0, n - 1, dispatch, 0)
    arr[me] = pack(me)

    slot = slot_t[...].T
    logits = lax.dot_general(
        tokens, router_ref[...], (((1,), (1,)), ((), ())), preferred_element_type=F32
    )
    lifted = jnp.where(slot >= 0.0, jax.nn.sigmoid(logits), 0.0)
    gate = lifted / jnp.sum(lifted, axis=1, keepdims=True)
    gate_hi = gate.astype(BF)
    gate_lo = (gate - gate_hi.astype(F32)).astype(BF)
    rows_all = experts * cap
    wide = lax.broadcasted_iota(jnp.int32, (experts, rows_all), 1)
    first = lax.broadcasted_iota(jnp.int32, (experts, rows_all), 0) * cap
    spread_e = ((wide >= first) & (wide < first + cap)).astype(BF)
    slot_all = jnp.dot(slot.astype(BF), spread_e, preferred_element_type=F32)
    place_all = (lax.broadcasted_iota(jnp.int32, (tok, rows_all), 1) % cap).astype(F32)
    here = slot_all == place_all
    hi_all = jnp.dot(gate_hi, spread_e, preferred_element_type=F32)
    lo_all = jnp.dot(gate_lo, spread_e, preferred_element_type=F32)
    mix[0] = jnp.where(here, hi_all, 0.0).astype(BF)
    mix[1] = jnp.where(here, lo_all, 0.0).astype(BF)

    for j, (i, rows) in enumerate(pieces):
        for t in range(chips - 1):
            g = peer(t)
            wait_bytes(weights.at[i, g, rows], w_peer.at[g // 2, j])
            piece = weights.at[i, g, rows]
            remote(piece, piece, f_send, f_recv, "grp", sib).start()
    for i in range(2):
        wait_bytes(weights.at[i, grp], w_local)
    wait_bytes(weights.at[:, pl.ds(0, 1)], w_sib)
    wait_bytes(weights.at[:, pl.ds(0, chips - 1)], f_recv)

    my_half = me // half
    far = 1 - my_half
    wait_bytes(arr.at[pl.ds(0, half)], d_recv.at[far])
    for step in range(2):
        side = far if step == 0 else my_half
        if step == 1:
            wait_bytes(arr.at[pl.ds(0, half - 1)], d_recv.at[my_half])
        block = pl.ds(side * half, half)

        def expert(g, carry, block=block):
            x = arr[block].reshape(half * cap, width)
            u = lax.dot_general(
                x, weights[0, g], (((1,), (1,)), ((), ())), preferred_element_type=F32
            )
            inner = math.sqrt(2.0 / math.pi) * (u + 0.044715 * (u * u * u))
            hidden = (0.5 * u * (1.0 + jnp.tanh(inner))).astype(BF)
            add = jnp.dot(hidden, weights[1, g], preferred_element_type=F32)
            acc[...] = jnp.where(g == 0, add, acc[...] + add)
            return carry

        acc[...] = jnp.zeros_like(acc)
        lax.fori_loop(0, n_grp, expert, 0)
        outcome = acc[...].astype(BF).reshape(half, cap, width)
        arr[block] = outcome
        for i in range(half):
            dst = side * half + (me + i) % half

            def go(dst=dst):
                remote(
                    arr.at[dst], back.at[me], r_send, r_recv.at[my_half], "seq", dst
                ).start()

            if step == 0:
                go()
            elif i > 0:
                go()
            else:
                back[me] = arr[me]

    for step in range(2):
        side = my_half if step == 0 else far
        count = half - 1 if step == 0 else half
        wait_bytes(back.at[pl.ds(0, count)], r_recv.at[side])
        rows = back[pl.ds(side * half, half)].reshape(half * cap, width)
        lanes = pl.ds(pl.multiple_of(side * (half * cap), half * cap), half * cap)
        add = jnp.dot(mix[0, :, lanes], rows, preferred_element_type=F32)
        add = add + jnp.dot(mix[1, :, lanes], rows, preferred_element_type=F32)
        moe[...] = add if step == 0 else moe[...] + add

    def finish(b, carry):
        m = mod_ref[b].astype(F32)
        rows = moe[pl.ds(pl.multiple_of(b * ld, ld), ld), :]
        out_ref[b] = (stream[b].astype(F32) + m[3:4] * rows).astype(BF)
        return carry

    lax.fori_loop(0, seqs, finish, 0)

    wait_bytes(qkv.at[:, :, pl.ds(0, (n - 1) * ld)], q_send)
    wait_bytes(att.at[pl.ds(0, (n - 1) * pc)], a_send)
    wait_bytes(outb.at[pl.ds(0, n - 1)], d_send)
    wait_bytes(back.at[pl.ds(0, n - 1)], r_send)
    wait_bytes(weights.at[:, pl.ds(0, chips)], w_send)
    wait_bytes(weights.at[:, pl.ds(0, chips - 1)], f_send)


def per_device(
    query_heads, key_heads, value_heads, residual, modulation, router, up_proj, down_proj,
    expert_ids,
):
    seqs, heads, ld, hd = query_heads.shape
    n = lax.axis_size("seq")
    n_grp = lax.axis_size("grp")
    pc = seqs * heads // n
    chunks = 3 if pc % 3 == 0 else 1
    tok = seqs * ld
    width = heads * hd
    experts = router.shape[1]
    cap = 4 * tok // experts
    ff = up_proj.shape[1]
    half = n // 2

    def arrange(array):
        return array.reshape(n, pc, ld, hd)

    ids = expert_ids.reshape(tok, 2)
    any_spec = pl.BlockSpec(memory_space=pltpu.HBM)
    vmem = pl.BlockSpec(memory_space=pltpu.VMEM)
    dma = pltpu.SemaphoreType.DMA
    return pl.pallas_call(
        functools.partial(layer_kernel, n, n_grp, chunks),
        out_shape=jax.ShapeDtypeStruct((seqs, ld, width), BF),
        in_specs=[any_spec] * 4 + [vmem] * 2 + [any_spec] * 2 + [vmem],
        out_specs=vmem,
        scratch_shapes=[
            pltpu.VMEM((seqs, ld, width), BF),
            pltpu.VMEM((3, pc, n * ld, hd), BF),
            pltpu.VMEM((pc, n * ld, hd), BF),
            pltpu.VMEM((n * pc, ld, hd), BF),
            pltpu.VMEM((seqs, ld, width), BF),
            pltpu.VMEM((seqs, ld, width), BF),
            pltpu.VMEM((experts, tok), F32),
            pltpu.VMEM((2, tok, experts * cap), BF),
            pltpu.VMEM((n, cap, width), BF),
            pltpu.VMEM((n, cap, width), BF),
            pltpu.VMEM((n, cap, width), BF),
            pltpu.VMEM((2, n_grp, ff, width), BF),
            pltpu.VMEM((half * cap, width), F32),
            pltpu.VMEM((tok, width), F32),
            dma, dma((chunks,)), dma, dma, dma, dma((2,)), dma, dma((2,)),
            dma, dma, dma((n_grp // 2, 4)), dma, dma, dma, dma,
        ],
        compiler_params=pltpu.CompilerParams(
            collective_id=0, has_side_effects=True, vmem_limit_bytes=56 * 1024 * 1024
        ),
    )(
        arrange(query_heads), arrange(key_heads), arrange(value_heads), residual, modulation,
        router.T, up_proj, down_proj, ids.T,
    )


def solution(mesh):
    return jax.shard_map(
        per_device,
        mesh=mesh,
        in_specs=(
            P("grp", None, "seq", None),
            P("grp", None, "seq", None),
            P("grp", None, "seq", None),
            P("grp", "seq", None),
            P("grp", None, None),
            P(),
            P("seq", "grp", None),
            P("seq", "grp", None),
            P("grp", "seq", None, None),
        ),
        out_specs=P("grp", "seq", None),
        check_vma=False,
    )
```
